256 devices in a mesh: major: 16 (over x, y), minor: 16 (over z, core).
Axes of the slice: x: 4, y: 4, z: 8, core: 2. Of those that a mesh axis runs over, the one named last changes fastest.
Arguments:
- context: bfloat16 [131072, 1024], P(('major', 'minor')), may hold values from -100 to 100
- latents: bfloat16 [2048, 1024], P('major'), may hold values from -6 to 6
- ends: int32 [2048], replicated, may hold values from 1 to 131072, as said below
- w_query: bfloat16 [1024, 1024], replicated, may hold values from -2 to 2
- w_key: bfloat16 [1024, 1024], replicated, may hold values from -1 to 1
- w_value: bfloat16 [1024, 1024], replicated, may hold values from -0.1875 to 0.1875
- w_out: bfloat16 [1024, 1024], P('minor'), may hold values from -1.5 to 1.5
Outputs:
- mixed: bfloat16 [2048, 1024], P(('major', 'minor'))
The draws below stay inside these ranges and needn't reach their ends.
Inputs may be any that keep to these rules, and one draw needn't show every extreme that they name: Latent row q attends context positions 0 to ends[q] - 1.
All inputs are finite; a program needn't handle non-finite values.
Results may differ from the reference program's by a relative error of at most 0.015.
The reference program's roundings to bfloat16 on the way (of `keys`, `values`, `queries`, `probs` and `attended`) count: a program that leaves them out, or rounds other values in their place, can miss the bound.
Values may be sent and summed in bfloat16 or wider, within the bound.
A program may use at most 128 MiB of HBM per device.

```python
import math
import jax
import jax.numpy as jnp
from jax import lax

HEADS = 16
HEAD = 64
D = 1024
LATENTS = 2048
TOK_DEV = 512
CTX = 131072
N_MAJOR = 16
N_MINOR = 16


def common_matrix(key):
    return jax.random.truncated_normal(jax.random.fold_in(key, 300), -4.0, 4.0, (D, D), jnp.float32)


def draw_context(key, part):
    base = jax.random.fold_in(key, 1)
    rows = jax.random.truncated_normal(base, -6.0, 6.0, (CTX, D), jnp.float32)
    return rows.astype(jnp.bfloat16)


def draw_latents(key, part):
    rows = jax.random.truncated_normal(jax.random.fold_in(key, 2), -6.0, 6.0, (LATENTS, D), jnp.float32)
    return rows.astype(jnp.bfloat16)


def draw_w_key(key, part):
    return (common_matrix(key) / math.sqrt(D)).astype(jnp.bfloat16)


def draw_w_query(key, part):
    fresh = jax.random.truncated_normal(jax.random.fold_in(key, 3), -4.0, 4.0, (D, D), jnp.float32)
    return (fresh * (2.45 / math.sqrt(D))).astype(jnp.bfloat16)


def draw_ends(key, part):
    key = jax.random.fold_in(key, 5)
    limits = jax.random.randint(key, (LATENTS,), 1, CTX + 1, jnp.int32)
    limits = limits.at[:4].set(CTX)
    return limits.at[4].set(1)


def steps_of(stream_key, shape, cuts, smallest, top_value):
    gain = 1.0
    for dim, blocks in cuts:
        heights = jax.random.uniform(jax.random.fold_in(jax.random.fold_in(stream_key, 6), dim), (blocks,), jnp.float32, smallest / len(cuts), top_value / len(cuts))
        gain = gain * jnp.repeat(jnp.exp(heights), shape[dim] // blocks).reshape((-1,) + (1,) * (len(shape) - 1 - dim))
    return gain


def centred(stream_key, extent, deviation, bound, split=(), kind=jnp.bfloat16):
    array = jax.random.normal(stream_key, extent, jnp.float32) * deviation
    if len(split) > 0:
        array = steps_of(stream_key, extent, split, -0.22, 0.18) * array
    return jnp.clip(array, min=-bound, max=bound).astype(kind)


def setup_inputs(seed: int = 0) -> dict:
    streams_of = jax.random.split(jax.random.key(seed), 8)
    return {
        "context": draw_context(jax.random.fold_in(streams_of[7], 71), 0),
        "latents": draw_latents(jax.random.fold_in(streams_of[7], 71), 0),
        "ends": draw_ends(jax.random.fold_in(streams_of[7], 71), 0),
        "w_query": draw_w_query(jax.random.fold_in(streams_of[7], 71), 0),
        "w_key": draw_w_key(jax.random.fold_in(streams_of[7], 71), 0),
        "w_value": centred(streams_of[5], (D, D), D ** -0.5, 0.1875),
        "w_out": centred(streams_of[6], (D, D), (max(D // 64, 1)) ** -0.5, 1.5, ((0, 16),)),
    }


def block_terms(query_heads, keys, values, ends, start):
    count = keys.shape[0]
    key_heads = keys.astype(jnp.float32).reshape(count, HEADS, HEAD)
    value_heads = values.astype(jnp.float32).reshape(count, HEADS, HEAD)
    scores = jnp.einsum("qhd,khd->qhk", query_heads, key_heads)
    places = start + jnp.arange(count, dtype=jnp.int32)
    live = places[None, :] < ends[:, None]
    scores = jnp.where(live[:, None, :], scores, -1e30)
    block_max = jnp.max(scores, axis=2)
    expon = jnp.exp(scores - block_max[:, :, None])
    block_sum = jnp.sum(expon, axis=2)
    probs = expon.astype(jnp.bfloat16).astype(jnp.float32)
    block_out = jnp.einsum("qhk,khd->qhd", probs, value_heads)
    return block_max, block_sum, block_out


def reference(context, latents, ends, w_query, w_key, w_value, w_out):
    queries = (jnp.dot(latents, w_query, preferred_element_type=jnp.float32) * (HEAD ** -0.5)).astype(jnp.bfloat16)
    query_heads = queries.astype(jnp.float32).reshape(LATENTS, HEADS, HEAD)
    nblocks = N_MAJOR * N_MINOR
    pieces = context.reshape(nblocks, TOK_DEV, D)

    def step(carry, item):
        top, numerator, denominator = carry
        rows, index = item
        keys = jnp.dot(rows, w_key, preferred_element_type=jnp.float32).astype(jnp.bfloat16)
        values = jnp.dot(rows, w_value, preferred_element_type=jnp.float32).astype(jnp.bfloat16)
        start = (index * TOK_DEV).astype(jnp.int32)
        block_max, block_sum, block_out = block_terms(query_heads, keys, values, ends, start)
        new_top = jnp.maximum(top, block_max)
        older = jnp.exp(top - new_top)
        fresh = jnp.exp(block_max - new_top)
        numerator = numerator * older[:, :, None] + block_out * fresh[:, :, None]
        denominator = denominator * older + block_sum * fresh
        return (new_top, numerator, denominator), None

    init = (jnp.full((LATENTS, HEADS), -3e30, jnp.float32),
            jnp.zeros((LATENTS, HEADS, HEAD), jnp.float32),
            jnp.zeros((LATENTS, HEADS), jnp.float32))
    final, unused = lax.scan(step, init, (pieces, jnp.arange(nblocks, dtype=jnp.int32)))
    top, numerator, denominator = final
    attended = (numerator / denominator[:, :, None]).reshape(LATENTS, D).astype(jnp.bfloat16)
    return jnp.dot(attended, w_out, preferred_element_type=jnp.float32).astype(jnp.bfloat16)
```

```python
import math

import jax
import jax.numpy as jnp
from jax import lax
from jax.experimental import pallas as pl
from jax.experimental.pallas import tpu as pltpu
from jax.sharding import PartitionSpec as P

HEAD = 64
NX, NY, NZ = 4, 4, 8
HEADS = 8
FEAT = HEADS * HEAD
PHASES = 2
GROUP = HEADS // PHASES
WIDE = GROUP * HEAD
TOK = 512
POS = 2 * TOK
ROWS = 128
OWN = 2 * 8
VROWS = 80
PAY = WIDE + 32
LOG2E = math.log2(math.e)
NEG = -1e30
MESH = pl.DeviceIdType.MESH
BF = jnp.bfloat16
F32 = jnp.float32


def split3(a):
    hi = a.astype(BF)
    rest = a - hi.astype(F32)
    mid = rest.astype(BF)
    low = (rest - mid.astype(F32)).astype(BF)
    return hi, mid, low


def stats_of(pay):
    rows = pay[WIDE:, :].astype(F32)
    return rows[:8] + rows[8:16] + rows[16:24]


def stats_rows(stats):
    terms = [t.astype(F32) for t in split3(stats)]
    return jnp.concatenate(terms + [jnp.zeros_like(stats)], axis=0)


def merge(pays):
    stats = [stats_of(pay) for pay in pays]
    top = stats[0][:GROUP]
    for st in stats[1:]:
        top = jnp.maximum(top, st[:GROUP])
    factors = [jnp.exp2(st[:GROUP] - top) for st in stats]
    den = sum(f * st[GROUP:] for f, st in zip(factors, stats))
    nums = []
    for h in range(GROUP):
        rows = slice(h * HEAD, h * HEAD + HEAD)
        nums.append(sum(pay[rows, :].astype(F32) * f[h : h + 1, :] for f, pay in zip(factors, pays)))
    return nums, jnp.concatenate([top, den], axis=0)


def write_payload(dst, nums, stats):
    for h in range(GROUP):
        dst[h * HEAD : h * HEAD + HEAD, :] = nums[h].astype(BF)
    dst[WIDE:, :] = stats_rows(stats).astype(BF)


def kernel(
    ctx_ref, lat_ref, ends_ref, wq_ref, wk_ref, wv_ref, wo_ref, out_ref,
    ctx, lat, wq, wk, wv, wo, qt, kk, vt, part, recv_x, sum_y, recv_y, zsend, zbuf, mix, mix_in, first_scores,
    load_sem, ctx_sem, wo_send, wo_recv, qx_send, qd_send, qy_send, q_recv,
    x_send, x_recv, y_send, y_recv, z_send, z_recv, core_sem,
):
    major, minor = lax.axis_index("major"), lax.axis_index("minor")
    x, y = lax.div(major, NY), lax.rem(major, NY)
    z, c = lax.div(minor, 2), lax.rem(minor, 2)

    def at_x(d):
        return (lax.rem(x + d, NX) * NY + y, minor)

    def at_y(d):
        return (x * NY + lax.rem(y + d, NY), minor)

    def at_xy(d, e):
        return (lax.rem(x + d, NX) * NY + lax.rem(y + e, NY), minor)

    other = (major, 2 * z + 1 - c)
    half = pl.ds(pl.multiple_of(c * FEAT, FEAT), FEAT)
    mine = pl.ds(pl.multiple_of(c * TOK, TOK), TOK)
    theirs = pl.ds(pl.multiple_of((1 - c) * TOK, TOK), TOK)

    loads = [
        pltpu.make_async_copy(lat_ref, lat, load_sem.at[0]),
        pltpu.make_async_copy(wq_ref.at[:, half], wq, load_sem.at[1]),
        pltpu.make_async_copy(ctx_ref, ctx.at[mine], load_sem.at[2]),
        pltpu.make_async_copy(wk_ref.at[:, half], wk, load_sem.at[3]),
        pltpu.make_async_copy(wv_ref.at[:, half], wv, load_sem.at[4]),
    ]
    for load in loads:
        load.start()

    barrier = pltpu.get_barrier_semaphore()
    for d in range(1, 4):
        pl.semaphore_signal(barrier, inc=1, device_id=at_x(d), device_id_type=MESH)
        pl.semaphore_signal(barrier, inc=1, device_id=at_y(d), device_id_type=MESH)
    for d in (1, 3):
        for e in (1, 3):
            pl.semaphore_signal(barrier, inc=1, device_id=at_xy(d, e), device_id_type=MESH)
    for d in range(1, 16):
        pl.semaphore_signal(barrier, inc=1, device_id=(major, lax.rem(minor + d, 16)), device_id_type=MESH)
    pl.semaphore_wait(barrier, 25)

    ctx_copy = pltpu.make_async_remote_copy(
        src_ref=ctx_ref, dst_ref=ctx.at[mine], send_sem=ctx_sem.at[0], recv_sem=ctx_sem.at[1],
        device_id=other, device_id_type=MESH,
    )
    ctx_copy.start()

    def q_block(xx, yy):
        return xx * NY + yy

    own = q_block(x, y)
    loads[0].wait()
    loads[1].wait()
    q = jnp.dot(lat[...], wq[...], preferred_element_type=F32) * HEAD ** (-0.5)
    q = jnp.transpose(q.astype(BF).astype(F32)).astype(BF)
    for g in range(PHASES):
        qt[g, own] = q[g * WIDE : (g + 1) * WIDE, :]

    def q_copy(g, block, send_sem, device):
        return pltpu.make_async_remote_copy(
            src_ref=qt.at[g, block], dst_ref=qt.at[g, block], send_sem=send_sem, recv_sem=q_recv.at[g, block],
            device_id=device, device_id_type=MESH,
        )

    def q_along_x(g, d):
        return q_copy(g, own, qx_send.at[g, d - 1], at_x(NX - d))

    def q_along_y(g, dx, d):
        return q_copy(g, q_block(lax.rem(x + dx, NX), y), qy_send.at[g, dx, d - 1], at_y(NY - d))

    def q_across(i, d):
        return q_copy(0, own, qd_send.at[i], at_xy(d, NY - 1))

    def q_wait(g, xx, yy):
        q_copy(g, q_block(xx, yy), qx_send.at[0, 0], other).wait_recv()

    q_along_y(0, 0, 1).start()
    q_along_x(0, 1).start()
    q_along_x(0, 3).start()
    q_across(0, 3).start()
    q_across(1, 1).start()
    q_along_y(0, 0, 2).start()
    q_along_y(0, 0, 3).start()
    q_along_x(0, 2).start()

    lane = lax.broadcasted_iota(jnp.int32, (TOK, 128), 1)

    def project_keys(rows):
        keys = jnp.dot(ctx[rows, :], wk[...], preferred_element_type=F32).astype(BF).astype(F32) * LOG2E
        hi = keys.astype(BF).astype(F32)
        low = (keys - hi).astype(BF).astype(F32)
        for pair in range(HEADS // 2):
            cols = slice(pair * 128, pair * 128 + 128)
            a, b = hi[:, cols], low[:, cols]
            even = jnp.where(lane < HEAD, a, pltpu.roll(b, HEAD, 1))
            odd = jnp.where(lane < HEAD, pltpu.roll(a, HEAD, 1), b)
            g, start = divmod(2 * pair, GROUP)
            kk[g, rows, start * 128 : start * 128 + 128] = even.astype(BF)
            kk[g, rows, start * 128 + 128 : start * 128 + 256] = odd.astype(BF)

    def project_values(rows):
        values = jnp.dot(ctx[rows, :], wv[...], preferred_element_type=F32).astype(BF).astype(F32)
        turned = jnp.transpose(values).astype(BF)
        for h in range(HEADS):
            g, i = divmod(h, GROUP)
            vt[g, i * VROWS : i * VROWS + HEAD, rows] = turned[h * HEAD : h * HEAD + HEAD, :]

    loads[2].wait()
    loads[3].wait()
    project_keys(mine)


    group, place = lax.div(minor, HEADS), lax.rem(minor, HEADS)
    wo_rows = pl.ds(pl.multiple_of(place * HEAD, HEAD), HEAD)

    def wo_copy(dz):
        return pltpu.make_async_remote_copy(
            src_ref=wo_ref, dst_ref=wo.at[wo_rows], send_sem=wo_send.at[dz], recv_sem=wo_recv.at[place],
            device_id=(major, lax.rem(z + dz, NZ) * 2 + group), device_id_type=MESH,
        )

    wo_local = pltpu.make_async_copy(wo_ref, wo.at[wo_rows], wo_recv.at[place])
    for dz in range(1, NZ):
        wo_copy(dz).start()

    @pl.when(c == group)
    def _():
        wo_local.start()

    @pl.when(c != group)
    def _():
        wo_copy(0).start()

    loads[4].wait()
    project_values(mine)
    row16 = lax.broadcasted_iota(jnp.int32, (16, POS), 0)
    for h in range(HEADS):
        g, i = divmod(h, GROUP)
        vt[g, i * VROWS + HEAD : (i + 1) * VROWS, :] = jnp.where(row16 == 0, 1.0, 0.0).astype(BF)

    ctx_copy.wait()
    project_keys(theirs)
    project_values(theirs)

    def x_copy(g, dx, yy):
        return pltpu.make_async_remote_copy(
            src_ref=part.at[g, q_block(lax.rem(x + dx, NX), yy)], dst_ref=recv_x.at[g, dx - 1, yy],
            send_sem=x_send.at[g, dx - 1, yy], recv_sem=x_recv.at[g, dx - 1, yy],
            device_id=at_x(dx), device_id_type=MESH,
        )

    def y_copy(g, dy):
        return pltpu.make_async_remote_copy(
            src_ref=sum_y.at[g, dy - 1], dst_ref=recv_y.at[g, dy - 1], send_sem=y_send.at[g, dy - 1],
            recv_sem=y_recv.at[g, dy - 1], device_id=at_y(dy), device_id_type=MESH,
        )

    def add_along_x(g, dy):
        yy = lax.rem(y + dy, NY)
        for d in range(1, 4):
            x_copy(g, d, yy).wait_recv()
        write_payload(sum_y.at[g, dy - 1], *merge([part.at[g, q_block(x, yy)]] + [recv_x.at[g, d, yy] for d in range(3)]))
        y_copy(g, dy).start()

    def z_rows(dz):
        return pl.ds(pl.multiple_of(lax.rem(z + dz, NZ) * OWN, OWN), OWN)

    def z_copy(g, dz):
        return pltpu.make_async_remote_copy(
            src_ref=zsend.at[g, z_rows(dz)], dst_ref=zbuf.at[g, z], send_sem=z_send.at[g, dz],
            recv_sem=z_recv.at[g, z], device_id=(major, lax.rem(z + dz, NZ) * 2 + c), device_id_type=MESH,
        )

    def add_along_y(g):
        for d in range(1, 4):
            x_copy(g, d, y).wait_recv()
        for d in range(1, 4):
            y_copy(g, d).wait_recv()
        nums, stats = merge(
            [part.at[g, own]] + [recv_x.at[g, d, y] for d in range(3)] + [recv_y.at[g, d] for d in range(3)]
        )
        zsend[g, :, :WIDE] = jnp.transpose(jnp.concatenate(nums, axis=0)).astype(BF)
        rows = jnp.concatenate([stats_rows(stats), jnp.zeros((96, ROWS), F32)], axis=0)
        zsend[g, :, WIDE:] = jnp.transpose(rows).astype(BF)
        for dz in range(1, NZ):
            z_copy(g, dz).start()
        pltpu.make_async_copy(zsend.at[g, z_rows(0)], zbuf.at[g, z], z_recv.at[g, z]).start()

    def add_along_z(g):
        head_of = lax.shift_right_logical(lax.broadcasted_iota(jnp.int32, (128, WIDE), 1), 6)
        line = lax.broadcasted_iota(jnp.int32, (128, WIDE), 0)
        spread = jnp.where(head_of == line, 1.0, 0.0).astype(BF)
        spread_den = jnp.where(head_of == line - GROUP, 1.0, 0.0).astype(BF)
        lane16 = lax.broadcasted_iota(jnp.int32, (OWN, 128), 1)
        for i in range(NZ):
            pltpu.make_async_copy(zsend.at[g, pl.ds(0, OWN)], zbuf.at[g, i], z_recv.at[g, i]).wait()
        sums = []
        for i in range(NZ):
            t = zbuf[g, i, :, WIDE:].astype(F32)
            sums.append(t + pltpu.roll(t, 120, 1) + pltpu.roll(t, 112, 1))
        top = sums[0]
        for t in sums[1:]:
            top = jnp.maximum(top, t)
        factors = [jnp.where(lane16 < GROUP, jnp.exp2(t - top), 0.0) for t in sums]
        wide = jnp.dot(jnp.concatenate(factors, axis=0).astype(BF), spread, preferred_element_type=F32)
        num = sum(wide[i * OWN : i * OWN + OWN] * zbuf[g, i, :, :WIDE].astype(F32) for i in range(NZ))
        den = sum(pltpu.roll(f, GROUP, 1) * t for f, t in zip(factors, sums))
        den_wide = sum(jnp.dot(t, spread_den, preferred_element_type=F32) for t in split3(den))
        attended = (num / den_wide).astype(BF)
        return jnp.dot(attended, wo[g * WIDE : (g + 1) * WIDE, :], preferred_element_type=F32)

    def wo_wait(i):
        pltpu.make_async_copy(wo_ref, wo.at[pl.ds(i * HEAD, HEAD)], wo_recv.at[i]).wait()

    base = (major * 16 + 2 * z) * TOK
    place_in_pos = lax.broadcasted_iota(jnp.int32, (POS, 2 * ROWS), 0)

    def scores(g, blocks, h):
        rows = slice(h * HEAD, h * HEAD + HEAD)
        qh = jnp.concatenate([qt[g, b, rows, :] for b in blocks], axis=1)
        qh = jnp.concatenate([qh, qh], axis=0)
        return jnp.dot(kk[g, :, h * 128 : h * 128 + 128], qh, preferred_element_type=F32)

    def attend(g, blocks, next_g, next_blocks):
        ends = jnp.concatenate([ends_ref[pl.ds(b, 1), :] for b in blocks], axis=1) - base
        live = place_in_pos < ends
        tops, dens = [], []
        ahead = first_scores[...]
        for h in range(GROUP):
            now = ahead
            if h + 1 < GROUP:
                ahead = scores(g, blocks, h + 1)
            else:
                first_scores[...] = scores(next_g, next_blocks, 0)
            now = jnp.where(live, now, NEG)
            top = jnp.ceil(jnp.max(now, axis=0, keepdims=True))
            probs = jnp.exp2(now - top).astype(BF)
            res = jnp.dot(vt[g, h * VROWS : (h + 1) * VROWS, :], probs, preferred_element_type=F32)
            for i, b in enumerate(blocks):
                part[g, b, h * HEAD : h * HEAD + HEAD, :] = res[:HEAD, i * ROWS : i * ROWS + ROWS].astype(BF)
            tops.append(top)
            dens.append(res[HEAD : HEAD + 1, :])
        rows = stats_rows(jnp.concatenate(tops + dens, axis=0)).astype(BF)
        for i, b in enumerate(blocks):
            part[g, b, WIDE:, :] = rows[:, i * ROWS : i * ROWS + ROWS]

    def plan(it):
        g, s = lax.div(it, 8), lax.rem(it, 8)
        early = jnp.where(g == 0, s < 2, s >= 6)
        t = jnp.where(g == 0, s + 4, s)
        k, second = lax.rem(t, 3), jnp.where(g == 0, lax.div(t - 6, 3), lax.div(t, 3))
        dx = jnp.where(g == 0, jnp.where(k == 2, 2, 1 + 2 * k), jnp.where(k == 0, 2, 2 * k - 1))
        dx = jnp.where(early, 0, dx)
        second = jnp.where(early, lax.rem(s, 2), second)
        xx = lax.rem(x + dx, NX)
        first = 2 * second + g
        dys = [first, lax.rem(first + 1, NY)]
        yys = [lax.rem(y + dy, NY) for dy in dys]
        return g, dx, xx, dys, yys

    def wait_queries(g, xx, dys, yys):
        for dy, yy in zip(dys, yys):

            @pl.when(dy != 0)
            def _():
                q_wait(g, xx, yy)

    def step(it, carry):
        g, dx, xx, dys, yys = plan(it)
        next_g, _, next_xx, next_dys, next_yys = plan(jnp.minimum(it + 1, 8 * PHASES - 1))

        @pl.when(it == 0)
        def _():
            for dx in (2, 1, 3):
                q_wait(0, lax.rem(x + dx, NX), y)
                for d in range(1 if dx == 2 else 2, 4):
                    q_along_y(0, dx, d).start()
            for d in (2, 1, 3):
                q_along_x(1, d).start()

        @pl.when(it == 3)
        def _():
            for dx in (2, 1, 3):
                q_wait(1, lax.rem(x + dx, NX), y)
                for d in range(1, 4):
                    q_along_y(1, dx, d).start()

        @pl.when(it == 5)
        def _():
            for d in range(1, 4):
                q_along_y(1, 0, d).start()

        @pl.when(it + 1 < 8 * PHASES)
        def _():
            wait_queries(next_g, next_xx, next_dys, next_yys)

        attend(g, [q_block(xx, yy) for yy in yys], next_g, [q_block(next_xx, yy) for yy in next_yys])

        @pl.when(dx != 0)
        def _():
            for yy in yys:
                x_copy(g, dx, yy).start()

        @pl.when((it == 9) | (it == 14))
        def _():
            for dy in (1, 2):
                add_along_x(lax.div(it - 9, 5), dy)

        @pl.when(it == 9)
        def _():
            add_along_x(0, 3)

        @pl.when(it == 13)
        def _():
            add_along_y(0)

        return carry

    q_wait(0, x, lax.rem(y + 1, NY))
    first_scores[...] = scores(0, [own, q_block(x, lax.rem(y + 1, NY))], 0)
    lax.fori_loop(0, 8 * PHASES, step, 0)

    add_along_x(1, 3)
    for i in range(HEADS):
        wo_wait(i)
    mix[...] = add_along_z(0)
    add_along_y(1)
    mix[...] += add_along_z(1)
    core_copy = pltpu.make_async_remote_copy(
        src_ref=mix.at[pl.ds(pl.multiple_of((1 - c) * 8, 8), 8)], dst_ref=mix_in,
        send_sem=core_sem.at[0], recv_sem=core_sem.at[1], device_id=other, device_id_type=MESH,
    )
    core_copy.start()

    q_across(0, 3).wait_send()
    q_across(1, 1).wait_send()
    for g in range(PHASES):
        for d in range(1, 4):
            q_along_x(g, d).wait_send()
            y_copy(g, d).wait_send()
            for yy in range(NY):
                x_copy(g, d, yy).wait_send()
            for dx in range(NX):
                if (g, d, dx % 2) != (0, 1, 1):
                    q_along_y(g, dx, d).wait_send()
        for dz in range(1, NZ):
            z_copy(g, dz).wait_send()
    for dz in range(1, NZ):
        wo_copy(dz).wait_send()

    @pl.when(c != group)
    def _():
        wo_copy(0).wait_send()

    core_copy.wait()
    out_ref[...] = (mix[pl.ds(pl.multiple_of(c * 8, 8), 8), :] + mix_in[...]).astype(BF)


def local(context, latents, ends, w_query, w_key, w_value, w_out):
    dma = pltpu.SemaphoreType.DMA
    vmem = pltpu.VMEM
    hbm = pl.BlockSpec(memory_space=pl.ANY)
    return pl.pallas_call(
        kernel,
        out_shape=jax.ShapeDtypeStruct((8, 2 * FEAT), BF),
        in_specs=[hbm, hbm, pl.BlockSpec(memory_space=vmem), hbm, hbm, hbm, hbm],
        out_specs=pl.BlockSpec(memory_space=vmem),
        scratch_shapes=[
            vmem((POS, 1024), BF),
            vmem((ROWS, 1024), BF),
            vmem((1024, FEAT), BF),
            vmem((1024, FEAT), BF),
            vmem((1024, FEAT), BF),
            vmem((FEAT, 1024), BF),
            vmem((PHASES, NX * NY, WIDE, ROWS), BF),
            vmem((PHASES, POS, 128 * GROUP), BF),
            vmem((PHASES, VROWS * GROUP, POS), BF),
            vmem((PHASES, NX * NY, PAY, ROWS), BF),
            vmem((PHASES, 3, NY, PAY, ROWS), BF),
            vmem((PHASES, 3, PAY, ROWS), BF),
            vmem((PHASES, 3, PAY, ROWS), BF),
            vmem((PHASES, ROWS, WIDE + 128), BF),
            vmem((PHASES, NZ, OWN, WIDE + 128), BF),
            vmem((OWN, 1024), F32),
            vmem((8, 1024), F32),
            vmem((POS, 2 * ROWS), F32),
            dma((5,)), dma((2,)), dma((NZ,)), dma((HEADS,)),
            dma((PHASES, 3)), dma((2,)), dma((PHASES, NX, 3)), dma((PHASES, NX * NY)),
            dma((PHASES, 3, NY)), dma((PHASES, 3, NY)), dma((PHASES, 3)), dma((PHASES, 3)),
            dma((PHASES, NZ)), dma((PHASES, NZ)), dma((2,)),
        ],
        compiler_params=pltpu.CompilerParams(
            collective_id=0, has_side_effects=True, vmem_limit_bytes=63 * 2**20
        ),
        name="attend",
    )(context, latents, ends.reshape(NX * NY, ROWS), w_query, w_key, w_value, w_out)


def solution(mesh):
    in_specs = (P(("major", "minor"), None), P("major", None), P(), P(), P(), P(), P("minor", None))
    out_specs = P(("major", "minor"), None)
    return jax.shard_map(local, mesh=mesh, in_specs=in_specs, out_specs=out_specs, check_vma=False)
```

```python
import math

import jax
import jax.numpy as jnp
from jax import lax
from jax.experimental import pallas as pl
from jax.experimental.pallas import tpu as pltpu
from jax.sharding import PartitionSpec as P

HEAD = 64
NX, NY, NZ = 4, 4, 8
HEADS = 8
FEAT = HEADS * HEAD
PHASES = 2
GROUP = HEADS // PHASES
WIDE = GROUP * HEAD
TOK = 512
POS = 2 * TOK
ROWS = 128
PART = 128
OWN = 2 * 8
VROWS = 80
PAY = WIDE + 32
LOG2E = math.log2(math.e)
NEG = -1e30
MESH = pl.DeviceIdType.MESH
BF = jnp.bfloat16
F32 = jnp.float32


def split3(a):
    hi = a.astype(BF)
    rest = a - hi.astype(F32)
    mid = rest.astype(BF)
    low = (rest - mid.astype(F32)).astype(BF)
    return hi, mid, low


def stats_of(pay):
    rows = pay[WIDE:, :].astype(F32)
    return rows[:8] + rows[8:16] + rows[16:24]


def stats_rows(stats):
    terms = [t.astype(F32) for t in split3(stats)]
    return jnp.concatenate(terms + [jnp.zeros_like(stats)], axis=0)


def merge(pays):
    stats = [stats_of(pay) for pay in pays]
    top = stats[0][:GROUP]
    for st in stats[1:]:
        top = jnp.maximum(top, st[:GROUP])
    factors = [jnp.exp2(st[:GROUP] - top) for st in stats]
    den = sum(f * st[GROUP:] for f, st in zip(factors, stats))
    nums = []
    for h in range(GROUP):
        rows = slice(h * HEAD, h * HEAD + HEAD)
        nums.append(sum(pay[rows, :].astype(F32) * f[h : h + 1, :] for f, pay in zip(factors, pays)))
    return nums, jnp.concatenate([top, den], axis=0)


def write_payload(dst, nums, stats):
    for h in range(GROUP):
        dst[h * HEAD : h * HEAD + HEAD, :] = nums[h].astype(BF)
    dst[WIDE:, :] = stats_rows(stats).astype(BF)


def kernel(
    ctx_ref, lat_ref, ends_ref, wq_ref, wk_ref, wv_ref, wo_ref, out_ref,
    ctx, lat, wq, wk, wv, wo, qt, kk, vt, part, recv_x, sum_y, recv_y, zsend, zbuf, mix, mix_in, held, first_top,
    load_sem, ctx_sem, wo_send, wo_recv, qx_send, qd_send, qy_send, q_recv,
    x_send, x_recv, y_send, y_recv, z_send, z_recv, core_sem,
):
    major, minor = lax.axis_index("major"), lax.axis_index("minor")
    x, y = lax.div(major, NY), lax.rem(major, NY)
    z, c = lax.div(minor, 2), lax.rem(minor, 2)

    def at_x(d):
        return (lax.rem(x + d, NX) * NY + y, minor)

    def at_y(d):
        return (x * NY + lax.rem(y + d, NY), minor)

    def at_xy(d, e):
        return (lax.rem(x + d, NX) * NY + lax.rem(y + e, NY), minor)

    other = (major, 2 * z + 1 - c)
    half = pl.ds(pl.multiple_of(c * FEAT, FEAT), FEAT)
    mine = pl.ds(pl.multiple_of(c * TOK, TOK), TOK)
    theirs = pl.ds(pl.multiple_of((1 - c) * TOK, TOK), TOK)

    loads = [
        pltpu.make_async_copy(lat_ref, lat, load_sem.at[0]),
        pltpu.make_async_copy(wq_ref.at[:, half], wq, load_sem.at[1]),
        pltpu.make_async_copy(ctx_ref, ctx.at[mine], load_sem.at[2]),
        pltpu.make_async_copy(wk_ref.at[:, half], wk, load_sem.at[3]),
        pltpu.make_async_copy(wv_ref.at[:, half], wv, load_sem.at[4]),
    ]
    for load in loads:
        load.start()

    barrier = pltpu.get_barrier_semaphore()
    for d in range(1, 4):
        pl.semaphore_signal(barrier, inc=1, device_id=at_x(d), device_id_type=MESH)
        pl.semaphore_signal(barrier, inc=1, device_id=at_y(d), device_id_type=MESH)
    for d in (1, 3):
        for e in (1, 3):
            pl.semaphore_signal(barrier, inc=1, device_id=at_xy(d, e), device_id_type=MESH)
    for d in range(1, 16):
        pl.semaphore_signal(barrier, inc=1, device_id=(major, lax.rem(minor + d, 16)), device_id_type=MESH)
    pl.semaphore_wait(barrier, 25)

    ctx_copy = pltpu.make_async_remote_copy(
        src_ref=ctx_ref, dst_ref=ctx.at[mine], send_sem=ctx_sem.at[0], recv_sem=ctx_sem.at[1],
        device_id=other, device_id_type=MESH,
    )
    ctx_copy.start()

    def q_block(xx, yy):
        return xx * NY + yy

    own = q_block(x, y)
    loads[0].wait()
    loads[1].wait()
    q = jnp.dot(lat[...], wq[...], preferred_element_type=F32) * HEAD ** (-0.5)
    q = jnp.transpose(q.astype(BF).astype(F32)).astype(BF)
    for g in range(PHASES):
        qt[g, own] = q[g * WIDE : (g + 1) * WIDE, :]

    def q_copy(g, block, send_sem, device):
        return pltpu.make_async_remote_copy(
            src_ref=qt.at[g, block], dst_ref=qt.at[g, block], send_sem=send_sem, recv_sem=q_recv.at[g, block],
            device_id=device, device_id_type=MESH,
        )

    def q_along_x(g, d):
        return q_copy(g, own, qx_send.at[g, d - 1], at_x(NX - d))

    def q_along_y(g, dx, d):
        return q_copy(g, q_block(lax.rem(x + dx, NX), y), qy_send.at[g, dx, d - 1], at_y(NY - d))

    def q_across(i, d):
        return q_copy(0, own, qd_send.at[i], at_xy(d, NY - 1))

    def q_wait(g, xx, yy):
        q_copy(g, q_block(xx, yy), qx_send.at[0, 0], other).wait_recv()

    q_along_y(0, 0, 1).start()
    q_along_x(0, 1).start()
    q_along_x(0, 3).start()
    q_across(0, 3).start()
    q_across(1, 1).start()
    q_along_y(0, 0, 2).start()
    q_along_y(0, 0, 3).start()
    q_along_x(0, 2).start()

    lane = lax.broadcasted_iota(jnp.int32, (TOK, 128), 1)

    def project_keys(rows):
        keys = jnp.dot(ctx[rows, :], wk[...], preferred_element_type=F32).astype(BF).astype(F32) * LOG2E
        hi = keys.astype(BF).astype(F32)
        low = (keys - hi).astype(BF).astype(F32)
        for pair in range(HEADS // 2):
            cols = slice(pair * 128, pair * 128 + 128)
            a, b = hi[:, cols], low[:, cols]
            even = jnp.where(lane < HEAD, a, pltpu.roll(b, HEAD, 1))
            odd = jnp.where(lane < HEAD, pltpu.roll(a, HEAD, 1), b)
            g, start = divmod(2 * pair, GROUP)
            kk[g, rows, start * 128 : start * 128 + 128] = even.astype(BF)
            kk[g, rows, start * 128 + 128 : start * 128 + 256] = odd.astype(BF)

    def project_values(rows):
        values = jnp.dot(ctx[rows, :], wv[...], preferred_element_type=F32).astype(BF).astype(F32)
        turned = jnp.transpose(values).astype(BF)
        for h in range(HEADS):
            g, i = divmod(h, GROUP)
            vt[g, i * VROWS : i * VROWS + HEAD, rows] = turned[h * HEAD : h * HEAD + HEAD, :]

    loads[2].wait()
    loads[3].wait()
    project_keys(mine)


    group, place = lax.div(minor, HEADS), lax.rem(minor, HEADS)
    wo_rows = pl.ds(pl.multiple_of(place * HEAD, HEAD), HEAD)

    def wo_copy(dz):
        return pltpu.make_async_remote_copy(
            src_ref=wo_ref, dst_ref=wo.at[wo_rows], send_sem=wo_send.at[dz], recv_sem=wo_recv.at[place],
            device_id=(major, lax.rem(z + dz, NZ) * 2 + group), device_id_type=MESH,
        )

    wo_local = pltpu.make_async_copy(wo_ref, wo.at[wo_rows], wo_recv.at[place])
    for dz in range(1, NZ):
        wo_copy(dz).start()

    @pl.when(c == group)
    def _():
        wo_local.start()

    @pl.when(c != group)
    def _():
        wo_copy(0).start()

    loads[4].wait()
    project_values(mine)
    row16 = lax.broadcasted_iota(jnp.int32, (16, POS), 0)
    for h in range(HEADS):
        g, i = divmod(h, GROUP)
        vt[g, i * VROWS + HEAD : (i + 1) * VROWS, :] = jnp.where(row16 == 0, 1.0, 0.0).astype(BF)

    ctx_copy.wait()
    project_keys(theirs)
    project_values(theirs)

    def x_copy(g, dx, yy):
        return pltpu.make_async_remote_copy(
            src_ref=part.at[g, q_block(lax.rem(x + dx, NX), yy)], dst_ref=recv_x.at[g, dx - 1, yy],
            send_sem=x_send.at[g, dx - 1, yy], recv_sem=x_recv.at[g, dx - 1, yy],
            device_id=at_x(dx), device_id_type=MESH,
        )

    def y_copy(g, dy):
        return pltpu.make_async_remote_copy(
            src_ref=sum_y.at[g, dy - 1], dst_ref=recv_y.at[g, dy - 1], send_sem=y_send.at[g, dy - 1],
            recv_sem=y_recv.at[g, dy - 1], device_id=at_y(dy), device_id_type=MESH,
        )

    def add_along_x(g, dy):
        yy = lax.rem(y + dy, NY)
        for d in range(1, 4):
            x_copy(g, d, yy).wait_recv()
        write_payload(sum_y.at[g, dy - 1], *merge([part.at[g, q_block(x, yy)]] + [recv_x.at[g, d, yy] for d in range(3)]))
        y_copy(g, dy).start()

    def z_rows(dz):
        return pl.ds(pl.multiple_of(lax.rem(z + dz, NZ) * OWN, OWN), OWN)

    def z_copy(g, dz):
        return pltpu.make_async_remote_copy(
            src_ref=zsend.at[g, z_rows(dz)], dst_ref=zbuf.at[g, z], send_sem=z_send.at[g, dz],
            recv_sem=z_recv.at[g, z], device_id=(major, lax.rem(z + dz, NZ) * 2 + c), device_id_type=MESH,
        )

    def add_along_y(g):
        for d in range(1, 4):
            x_copy(g, d, y).wait_recv()
        for d in range(1, 4):
            y_copy(g, d).wait_recv()
        nums, stats = merge(
            [part.at[g, own]] + [recv_x.at[g, d, y] for d in range(3)] + [recv_y.at[g, d] for d in range(3)]
        )
        zsend[g, :, :WIDE] = jnp.transpose(jnp.concatenate(nums, axis=0)).astype(BF)
        rows = jnp.concatenate([stats_rows(stats), jnp.zeros((96, ROWS), F32)], axis=0)
        zsend[g, :, WIDE:] = jnp.transpose(rows).astype(BF)
        for dz in (4, 3, 5, 2, 6, 1, 7):
            z_copy(g, dz).start()
        pltpu.make_async_copy(zsend.at[g, z_rows(0)], zbuf.at[g, z], z_recv.at[g, z]).start()

    def add_along_z(g):
        head_of = lax.shift_right_logical(lax.broadcasted_iota(jnp.int32, (128, WIDE), 1), 6)
        line = lax.broadcasted_iota(jnp.int32, (128, WIDE), 0)
        spread = jnp.where(head_of == line, 1.0, 0.0).astype(BF)
        spread_den = jnp.where(head_of == line - GROUP, 1.0, 0.0).astype(BF)
        lane16 = lax.broadcasted_iota(jnp.int32, (OWN, 128), 1)
        for i in range(NZ):
            pltpu.make_async_copy(zsend.at[g, pl.ds(0, OWN)], zbuf.at[g, i], z_recv.at[g, i]).wait()
        sums = []
        for i in range(NZ):
            t = zbuf[g, i, :, WIDE:].astype(F32)
            sums.append(t + pltpu.roll(t, 120, 1) + pltpu.roll(t, 112, 1))
        top = sums[0]
        for t in sums[1:]:
            top = jnp.maximum(top, t)
        factors = [jnp.where(lane16 < GROUP, jnp.exp2(t - top), 0.0) for t in sums]
        wide = jnp.dot(jnp.concatenate(factors, axis=0).astype(BF), spread, preferred_element_type=F32)
        num = sum(wide[i * OWN : i * OWN + OWN] * zbuf[g, i, :, :WIDE].astype(F32) for i in range(NZ))
        den = sum(pltpu.roll(f, GROUP, 1) * t for f, t in zip(factors, sums))
        den_wide = sum(jnp.dot(t, spread_den, preferred_element_type=F32) for t in split3(den))
        attended = (num / den_wide).astype(BF)
        return jnp.dot(attended, wo[g * WIDE : (g + 1) * WIDE, :], preferred_element_type=F32)

    def wo_wait(i):
        pltpu.make_async_copy(wo_ref, wo.at[pl.ds(i * HEAD, HEAD)], wo_recv.at[i]).wait()

    base = (major * 16 + 2 * z) * TOK
    place_in_part = lax.broadcasted_iota(jnp.int32, (PART, 2 * ROWS), 0)

    def scores(g, blocks, h, slot):
        ends = jnp.concatenate([ends_ref[pl.ds(b, 1), :] for b in blocks], axis=1) - base
        rows = slice(h * HEAD, h * HEAD + HEAD)
        qh = jnp.concatenate([qt[g, b, rows, :] for b in blocks], axis=1)
        qh = jnp.concatenate([qh, qh], axis=0)
        top = None
        for j in range(0, POS, PART):
            keys = kk[g, j : j + PART, h * 128 : h * 128 + 128]
            now = jnp.dot(keys, qh, preferred_element_type=F32)
            now = jnp.where(place_in_part < ends - j, now, NEG)
            held[slot, j : j + PART, :] = now
            most = jnp.max(now.reshape(PART // 8, 8, 2 * ROWS), axis=0)
            top = most if top is None else jnp.maximum(top, most)
        return jnp.ceil(jnp.max(top, axis=0, keepdims=True))

    def attend(g, blocks, next_g, next_blocks):
        tops, dens = [], []
        top = first_top[...]
        for h in range(GROUP):
            if h + 1 < GROUP:
                next_top = scores(g, blocks, h + 1, (h + 1) % 2)
            else:
                next_top = scores(next_g, next_blocks, 0, 0)
                first_top[...] = next_top
            probs = [
                jnp.exp2(held[h % 2, j : j + PART, :] - top).astype(BF) for j in range(0, POS, PART)
            ]
            probs = jnp.concatenate(probs, axis=0)
            res = jnp.dot(vt[g, h * VROWS : (h + 1) * VROWS, :], probs, preferred_element_type=F32)
            for i, b in enumerate(blocks):
                part[g, b, h * HEAD : h * HEAD + HEAD, :] = res[:HEAD, i * ROWS : i * ROWS + ROWS].astype(BF)
            tops.append(top)
            dens.append(res[HEAD : HEAD + 1, :])
            top = next_top
        rows = stats_rows(jnp.concatenate(tops + dens, axis=0)).astype(BF)
        for i, b in enumerate(blocks):
            part[g, b, WIDE:, :] = rows[:, i * ROWS : i * ROWS + ROWS]

    def plan(it):
        g, s = lax.div(it, 8), lax.rem(it, 8)
        early = jnp.where(g == 0, s < 2, s >= 6)
        t = jnp.where(g == 0, s + 4, s)
        k, second = lax.rem(t, 3), jnp.where(g == 0, lax.div(t - 6, 3), lax.div(t, 3))
        dx = jnp.where(g == 0, jnp.where(k == 2, 2, 1 + 2 * k), jnp.where(k == 0, 2, 2 * k - 1))
        dx = jnp.where(early, 0, dx)
        second = jnp.where(early, lax.rem(s, 2), second)
        xx = lax.rem(x + dx, NX)
        first = 2 * second + g
        dys = [first, lax.rem(first + 1, NY)]
        yys = [lax.rem(y + dy, NY) for dy in dys]
        return g, dx, xx, dys, yys

    def wait_queries(g, xx, dys, yys):
        for dy, yy in zip(dys, yys):

            @pl.when(dy != 0)
            def _():
                q_wait(g, xx, yy)

    def step(it, carry):
        g, dx, xx, dys, yys = plan(it)
        next_g, _, next_xx, next_dys, next_yys = plan(jnp.minimum(it + 1, 8 * PHASES - 1))

        @pl.when(it == 0)
        def _():
            for dx in (2, 1, 3):
                q_wait(0, lax.rem(x + dx, NX), y)
                for d in range(1 if dx == 2 else 2, 4):
                    q_along_y(0, dx, d).start()
            for d in (2, 1, 3):
                q_along_x(1, d).start()

        @pl.when(it == 3)
        def _():
            for dx in (2, 1, 3):
                q_wait(1, lax.rem(x + dx, NX), y)
                for d in range(1, 4):
                    q_along_y(1, dx, d).start()

        @pl.when(it == 5)
        def _():
            for d in range(1, 4):
                q_along_y(1, 0, d).start()

        @pl.when(it + 1 < 8 * PHASES)
        def _():
            wait_queries(next_g, next_xx, next_dys, next_yys)

        attend(g, [q_block(xx, yy) for yy in yys], next_g, [q_block(next_xx, yy) for yy in next_yys])

        @pl.when(dx != 0)
        def _():
            for yy in yys:
                x_copy(g, dx, yy).start()

        @pl.when((it == 9) | (it == 14))
        def _():
            for dy in (1, 2):
                add_along_x(lax.div(it - 9, 5), dy)

        @pl.when(it == 9)
        def _():
            add_along_x(0, 3)

        @pl.when(it == 13)
        def _():
            add_along_y(0)

        return carry

    q_wait(0, x, lax.rem(y + 1, NY))
    first_top[...] = scores(0, [own, q_block(x, lax.rem(y + 1, NY))], 0, 0)
    lax.fori_loop(0, 8 * PHASES, step, 0)

    add_along_x(1, 3)
    for i in range(HEADS):
        wo_wait(i)
    mix[...] = add_along_z(0)
    add_along_y(1)
    mix[...] += add_along_z(1)
    core_copy = pltpu.make_async_remote_copy(
        src_ref=mix.at[pl.ds(pl.multiple_of((1 - c) * 8, 8), 8)], dst_ref=mix_in,
        send_sem=core_sem.at[0], recv_sem=core_sem.at[1], device_id=other, device_id_type=MESH,
    )
    core_copy.start()

    q_across(0, 3).wait_send()
    q_across(1, 1).wait_send()
    for g in range(PHASES):
        for d in range(1, 4):
            q_along_x(g, d).wait_send()
            y_copy(g, d).wait_send()
            for yy in range(NY):
                x_copy(g, d, yy).wait_send()
            for dx in range(NX):
                if (g, d, dx % 2) != (0, 1, 1):
                    q_along_y(g, dx, d).wait_send()
        for dz in range(1, NZ):
            z_copy(g, dz).wait_send()
    for dz in range(1, NZ):
        wo_copy(dz).wait_send()

    @pl.when(c != group)
    def _():
        wo_copy(0).wait_send()

    core_copy.wait()
    out_ref[...] = (mix[pl.ds(pl.multiple_of(c * 8, 8), 8), :] + mix_in[...]).astype(BF)


def local(context, latents, ends, w_query, w_key, w_value, w_out):
    dma = pltpu.SemaphoreType.DMA
    vmem = pltpu.VMEM
    hbm = pl.BlockSpec(memory_space=pl.ANY)
    return pl.pallas_call(
        kernel,
        out_shape=jax.ShapeDtypeStruct((8, 2 * FEAT), BF),
        in_specs=[hbm, hbm, pl.BlockSpec(memory_space=vmem), hbm, hbm, hbm, hbm],
        out_specs=pl.BlockSpec(memory_space=vmem),
        scratch_shapes=[
            vmem((POS, 1024), BF),
            vmem((ROWS, 1024), BF),
            vmem((1024, FEAT), BF),
            vmem((1024, FEAT), BF),
            vmem((1024, FEAT), BF),
            vmem((FEAT, 1024), BF),
            vmem((PHASES, NX * NY, WIDE, ROWS), BF),
            vmem((PHASES, POS, 128 * GROUP), BF),
            vmem((PHASES, VROWS * GROUP, POS), BF),
            vmem((PHASES, NX * NY, PAY, ROWS), BF),
            vmem((PHASES, 3, NY, PAY, ROWS), BF),
            vmem((PHASES, 3, PAY, ROWS), BF),
            vmem((PHASES, 3, PAY, ROWS), BF),
            vmem((PHASES, ROWS, WIDE + 128), BF),
            vmem((PHASES, NZ, OWN, WIDE + 128), BF),
            vmem((OWN, 1024), F32),
            vmem((8, 1024), F32),
            vmem((2, POS, 2 * ROWS), F32),
            vmem((1, 2 * ROWS), F32),
            dma((5,)), dma((2,)), dma((NZ,)), dma((HEADS,)),
            dma((PHASES, 3)), dma((2,)), dma((PHASES, NX, 3)), dma((PHASES, NX * NY)),
            dma((PHASES, 3, NY)), dma((PHASES, 3, NY)), dma((PHASES, 3)), dma((PHASES, 3)),
            dma((PHASES, NZ)), dma((PHASES, NZ)), dma((2,)),
        ],
        compiler_params=pltpu.CompilerParams(
            collective_id=0, has_side_effects=True, vmem_limit_bytes=63 * 2**20
        ),
        name="attend",
    )(context, latents, ends.reshape(NX * NY, ROWS), w_query, w_key, w_value, w_out)


def solution(mesh):
    in_specs = (P(("major", "minor"), None), P("major", None), P(), P(), P(), P(), P("minor", None))
    out_specs = P(("major", "minor"), None)
    return jax.shard_map(local, mesh=mesh, in_specs=in_specs, out_specs=out_specs, check_vma=False)
```

```python
import math

import jax
import jax.numpy as jnp
from jax import lax
from jax.experimental import pallas as pl
from jax.experimental.pallas import tpu as pltpu
from jax.sharding import PartitionSpec as P

HEAD = 64
NX, NY, NZ = 4, 4, 8
HEADS = 8
FEAT = HEADS * HEAD
PHASES = 2
GROUP = HEADS // PHASES
WIDE = GROUP * HEAD
TOK = 512
POS = 2 * TOK
ROWS = 128
PART = 128
OWN = 2 * 8
VROWS = 80
PAY = WIDE + 16
LOG2E = math.log2(math.e)
NEG = -1e30
MESH = pl.DeviceIdType.MESH
BF = jnp.bfloat16
F32 = jnp.float32


def split3(a):
    hi = a.astype(BF)
    rest = a - hi.astype(F32)
    mid = rest.astype(BF)
    low = (rest - mid.astype(F32)).astype(BF)
    return hi, mid, low


def stats_of(pay):
    rows = pay[WIDE:, :].astype(F32)
    top = rows[:GROUP] + rows[GROUP : 2 * GROUP] + rows[2 * GROUP : 3 * GROUP]
    return jnp.concatenate([top, rows[3 * GROUP :]], axis=0)


def stats_rows(stats):
    terms = [t.astype(F32) for t in split3(stats[:GROUP])]
    return jnp.concatenate(terms + [stats[GROUP:]], axis=0)


def merge(pays):
    stats = [stats_of(pay) for pay in pays]
    top = stats[0][:GROUP]
    for st in stats[1:]:
        top = jnp.maximum(top, st[:GROUP])
    factors = [jnp.exp2(st[:GROUP] - top) for st in stats]
    den = sum(f * st[GROUP:] for f, st in zip(factors, stats))
    nums = []
    for h in range(GROUP):
        rows = slice(h * HEAD, h * HEAD + HEAD)
        nums.append(sum(pay[rows, :].astype(F32) * f[h : h + 1, :] for f, pay in zip(factors, pays)))
    return nums, jnp.concatenate([top, den], axis=0)


def write_payload(dst, nums, stats):
    for h in range(GROUP):
        dst[h * HEAD : h * HEAD + HEAD, :] = nums[h].astype(BF)
    dst[WIDE:, :] = stats_rows(stats).astype(BF)


def kernel(
    ctx_ref, lat_ref, ends_ref, wq_ref, wk_ref, wv_ref, wo_ref, out_ref,
    ctx, lat, wq, wk, wv, wo, qt, kk, vt, part, recv_x, sum_y, recv_y, zsend, zbuf, mix, mix_in, held, first_top,
    load_sem, ctx_sem, wo_send, wo_recv, qx_send, qd_send, qy_send, q_recv,
    x_send, x_recv, y_send, y_recv, z_send, z_recv, core_sem,
):
    major, minor = lax.axis_index("major"), lax.axis_index("minor")
    x, y = lax.div(major, NY), lax.rem(major, NY)
    z, c = lax.div(minor, 2), lax.rem(minor, 2)

    def at_x(d):
        return (lax.rem(x + d, NX) * NY + y, minor)

    def at_y(d):
        return (x * NY + lax.rem(y + d, NY), minor)

    def at_xy(d, e):
        return (lax.rem(x + d, NX) * NY + lax.rem(y + e, NY), minor)

    other = (major, 2 * z + 1 - c)
    half = pl.ds(pl.multiple_of(c * FEAT, FEAT), FEAT)
    mine = pl.ds(pl.multiple_of(c * TOK, TOK), TOK)
    theirs = pl.ds(pl.multiple_of((1 - c) * TOK, TOK), TOK)

    loads = [
        pltpu.make_async_copy(lat_ref, lat, load_sem.at[0]),
        pltpu.make_async_copy(wq_ref.at[:, half], wq, load_sem.at[1]),
        pltpu.make_async_copy(ctx_ref, ctx.at[mine], load_sem.at[2]),
        pltpu.make_async_copy(wk_ref.at[:, half], wk, load_sem.at[3]),
        pltpu.make_async_copy(wv_ref.at[:, half], wv, load_sem.at[4]),
    ]
    for load in loads:
        load.start()

    barrier = pltpu.get_barrier_semaphore()
    for d in range(1, 4):
        pl.semaphore_signal(barrier, inc=1, device_id=at_x(d), device_id_type=MESH)
        pl.semaphore_signal(barrier, inc=1, device_id=at_y(d), device_id_type=MESH)
    for d in (1, 3):
        for e in (1, 3):
            pl.semaphore_signal(barrier, inc=1, device_id=at_xy(d, e), device_id_type=MESH)
    for d in range(1, 16):
        pl.semaphore_signal(barrier, inc=1, device_id=(major, lax.rem(minor + d, 16)), device_id_type=MESH)

    def q_block(xx, yy):
        return xx * NY + yy

    own = q_block(x, y)
    loads[0].wait()
    loads[1].wait()
    q = jnp.dot(lat[...], wq[...], preferred_element_type=F32) * HEAD ** (-0.5)
    q = jnp.transpose(q.astype(BF).astype(F32)).astype(BF)
    for g in range(PHASES):
        qt[g, own] = q[g * WIDE : (g + 1) * WIDE, :]

    pl.semaphore_wait(barrier, 25)
    ctx_copy = pltpu.make_async_remote_copy(
        src_ref=ctx_ref, dst_ref=ctx.at[mine], send_sem=ctx_sem.at[0], recv_sem=ctx_sem.at[1],
        device_id=other, device_id_type=MESH,
    )
    ctx_copy.start()

    def q_copy(g, block, send_sem, device):
        return pltpu.make_async_remote_copy(
            src_ref=qt.at[g, block], dst_ref=qt.at[g, block], send_sem=send_sem, recv_sem=q_recv.at[g, block],
            device_id=device, device_id_type=MESH,
        )

    def q_along_x(g, d):
        return q_copy(g, own, qx_send.at[g, d - 1], at_x(NX - d))

    def q_along_y(g, dx, d):
        return q_copy(g, q_block(lax.rem(x + dx, NX), y), qy_send.at[g, dx, d - 1], at_y(NY - d))

    def q_across(i, d):
        return q_copy(0, own, qd_send.at[i], at_xy(d, NY - 1))

    def q_wait(g, xx, yy):
        q_copy(g, q_block(xx, yy), qx_send.at[0, 0], other).wait_recv()

    q_along_y(0, 0, 1).start()
    q_along_x(0, 1).start()
    q_along_x(0, 3).start()
    q_across(0, 3).start()
    q_across(1, 1).start()
    q_along_y(0, 0, 2).start()
    q_along_y(0, 0, 3).start()
    q_along_x(0, 2).start()

    lane = lax.broadcasted_iota(jnp.int32, (TOK, 128), 1)

    def project_keys(rows):
        keys = jnp.dot(ctx[rows, :], wk[...], preferred_element_type=F32).astype(BF).astype(F32) * LOG2E
        hi = keys.astype(BF).astype(F32)
        low = (keys - hi).astype(BF).astype(F32)
        for pair in range(HEADS // 2):
            cols = slice(pair * 128, pair * 128 + 128)
            a, b = hi[:, cols], low[:, cols]
            even = jnp.where(lane < HEAD, a, pltpu.roll(b, HEAD, 1))
            odd = jnp.where(lane < HEAD, pltpu.roll(a, HEAD, 1), b)
            g, start = divmod(2 * pair, GROUP)
            kk[g, rows, start * 128 : start * 128 + 128] = even.astype(BF)
            kk[g, rows, start * 128 + 128 : start * 128 + 256] = odd.astype(BF)

    def project_values(rows):
        values = jnp.dot(ctx[rows, :], wv[...], preferred_element_type=F32).astype(BF).astype(F32)
        turned = jnp.transpose(values).astype(BF)
        for h in range(HEADS):
            g, i = divmod(h, GROUP)
            vt[g, i * VROWS : i * VROWS + HEAD, rows] = turned[h * HEAD : h * HEAD + HEAD, :]

    loads[2].wait()
    loads[3].wait()
    project_keys(mine)


    group, place = lax.div(minor, HEADS), lax.rem(minor, HEADS)
    wo_rows = pl.ds(pl.multiple_of(place * HEAD, HEAD), HEAD)

    def wo_copy(dz):
        return pltpu.make_async_remote_copy(
            src_ref=wo_ref, dst_ref=wo.at[wo_rows], send_sem=wo_send.at[dz], recv_sem=wo_recv.at[place],
            device_id=(major, lax.rem(z + dz, NZ) * 2 + group), device_id_type=MESH,
        )

    wo_local = pltpu.make_async_copy(wo_ref, wo.at[wo_rows], wo_recv.at[place])
    for dz in range(1, NZ):
        wo_copy(dz).start()

    @pl.when(c == group)
    def _():
        wo_local.start()

    @pl.when(c != group)
    def _():
        wo_copy(0).start()

    loads[4].wait()
    project_values(mine)
    row16 = lax.broadcasted_iota(jnp.int32, (16, POS), 0)
    for h in range(HEADS):
        g, i = divmod(h, GROUP)
        vt[g, i * VROWS + HEAD : (i + 1) * VROWS, :] = jnp.where(row16 == 0, 1.0, 0.0).astype(BF)

    ctx_copy.wait()
    project_keys(theirs)
    project_values(theirs)

    def x_copy(g, dx, yy):
        return pltpu.make_async_remote_copy(
            src_ref=part.at[g, q_block(lax.rem(x + dx, NX), yy)], dst_ref=recv_x.at[g, dx - 1, yy],
            send_sem=x_send.at[g, dx - 1, yy], recv_sem=x_recv.at[g, dx - 1, yy],
            device_id=at_x(dx), device_id_type=MESH,
        )

    def y_copy(g, dy):
        return pltpu.make_async_remote_copy(
            src_ref=sum_y.at[g, dy - 1], dst_ref=recv_y.at[g, dy - 1], send_sem=y_send.at[g, dy - 1],
            recv_sem=y_recv.at[g, dy - 1], device_id=at_y(dy), device_id_type=MESH,
        )

    def add_along_x(g, dy):
        yy = lax.rem(y + dy, NY)
        for d in range(1, 4):
            x_copy(g, d, yy).wait_recv()
        write_payload(sum_y.at[g, dy - 1], *merge([part.at[g, q_block(x, yy)]] + [recv_x.at[g, d, yy] for d in range(3)]))
        y_copy(g, dy).start()

    def z_rows(dz):
        return pl.ds(pl.multiple_of(lax.rem(z + dz, NZ) * OWN, OWN), OWN)

    def z_copy(g, dz):
        return pltpu.make_async_remote_copy(
            src_ref=zsend.at[g, z_rows(dz)], dst_ref=zbuf.at[g, z], send_sem=z_send.at[g, dz],
            recv_sem=z_recv.at[g, z], device_id=(major, lax.rem(z + dz, NZ) * 2 + c), device_id_type=MESH,
        )

    def add_along_y(g):
        for d in range(1, 4):
            x_copy(g, d, y).wait_recv()
        for d in range(1, 4):
            y_copy(g, d).wait_recv()
        nums, stats = merge(
            [part.at[g, own]] + [recv_x.at[g, d, y] for d in range(3)] + [recv_y.at[g, d] for d in range(3)]
        )
        zsend[g, :, :WIDE] = jnp.transpose(jnp.concatenate(nums, axis=0)).astype(BF)
        rows = jnp.concatenate([stats_rows(stats), jnp.zeros((112, ROWS), F32)], axis=0)
        zsend[g, :, WIDE:] = jnp.transpose(rows).astype(BF)
        for dz in (4, 3, 5, 2, 6, 1, 7):
            z_copy(g, dz).start()
        pltpu.make_async_copy(zsend.at[g, z_rows(0)], zbuf.at[g, z], z_recv.at[g, z]).start()

    def add_along_z(g):
        head_of = lax.shift_right_logical(lax.broadcasted_iota(jnp.int32, (128, WIDE), 1), 6)
        line = lax.broadcasted_iota(jnp.int32, (128, WIDE), 0)
        spread = jnp.where(head_of == line, 1.0, 0.0).astype(BF)
        spread_den = jnp.where(head_of == line - 3 * GROUP, 1.0, 0.0).astype(BF)
        lane16 = lax.broadcasted_iota(jnp.int32, (OWN, 128), 1)
        for i in range(NZ):
            pltpu.make_async_copy(zsend.at[g, pl.ds(0, OWN)], zbuf.at[g, i], z_recv.at[g, i]).wait()
        sums = [zbuf[g, i, :, WIDE:].astype(F32) for i in range(NZ)]
        tops = [t + pltpu.roll(t, 128 - GROUP, 1) + pltpu.roll(t, 128 - 2 * GROUP, 1) for t in sums]
        top = tops[0]
        for t in tops[1:]:
            top = jnp.maximum(top, t)
        factors = [jnp.where(lane16 < GROUP, jnp.exp2(t - top), 0.0) for t in tops]
        wide = jnp.dot(jnp.concatenate(factors, axis=0).astype(BF), spread, preferred_element_type=F32)
        num = sum(wide[i * OWN : i * OWN + OWN] * zbuf[g, i, :, :WIDE].astype(F32) for i in range(NZ))
        den = sum(pltpu.roll(f, 3 * GROUP, 1) * t for f, t in zip(factors, sums))
        den_wide = sum(jnp.dot(t, spread_den, preferred_element_type=F32) for t in split3(den))
        attended = (num / den_wide).astype(BF)
        return jnp.dot(attended, wo[g * WIDE : (g + 1) * WIDE, :], preferred_element_type=F32)

    def wo_wait(i):
        pltpu.make_async_copy(wo_ref, wo.at[pl.ds(i * HEAD, HEAD)], wo_recv.at[i]).wait()

    base = (major * 16 + 2 * z) * TOK
    place_in_part = lax.broadcasted_iota(jnp.int32, (PART, 2 * ROWS), 0)

    def scores(g, blocks, h, slot):
        ends = jnp.concatenate([ends_ref[pl.ds(b, 1), :] for b in blocks], axis=1) - base
        rows = slice(h * HEAD, h * HEAD + HEAD)
        qh = jnp.concatenate([qt[g, b, rows, :] for b in blocks], axis=1)
        qh = jnp.concatenate([qh, qh], axis=0)
        top = None
        for j in range(0, POS, PART):
            keys = kk[g, j : j + PART, h * 128 : h * 128 + 128]
            now = jnp.dot(keys, qh, preferred_element_type=F32)
            now = jnp.where(place_in_part < ends - j, now, NEG)
            held[slot, j : j + PART, :] = now
            most = jnp.max(now.reshape(PART // 8, 8, 2 * ROWS), axis=0)
            top = most if top is None else jnp.maximum(top, most)
        return jnp.ceil(jnp.max(top, axis=0, keepdims=True))

    def attend(g, blocks, next_g, next_blocks):
        tops, dens = [], []
        top = first_top[...]
        for h in range(GROUP):
            if h + 1 < GROUP:
                next_top = scores(g, blocks, h + 1, (h + 1) % 2)
            else:
                next_top = scores(next_g, next_blocks, 0, 0)
                first_top[...] = next_top
            probs = [
                jnp.exp2(held[h % 2, j : j + PART, :] - top).astype(BF) for j in range(0, POS, PART)
            ]
            probs = jnp.concatenate(probs, axis=0)
            res = jnp.dot(vt[g, h * VROWS : (h + 1) * VROWS, :], probs, preferred_element_type=F32)
            for i, b in enumerate(blocks):
                part[g, b, h * HEAD : h * HEAD + HEAD, :] = res[:HEAD, i * ROWS : i * ROWS + ROWS].astype(BF)
            tops.append(top)
            dens.append(res[HEAD : HEAD + 1, :])
            top = next_top
        rows = stats_rows(jnp.concatenate(tops + dens, axis=0)).astype(BF)
        for i, b in enumerate(blocks):
            part[g, b, WIDE:, :] = rows[:, i * ROWS : i * ROWS + ROWS]

    def plan(it):
        g, s = lax.div(it, 8), lax.rem(it, 8)
        early = jnp.where(g == 0, s < 2, s >= 6)
        t = jnp.where(g == 0, s + 4, s)
        k, second = lax.rem(t, 3), jnp.where(g == 0, lax.div(t - 6, 3), lax.div(t, 3))
        dx = jnp.where(g == 0, jnp.where(k == 2, 2, 1 + 2 * k), jnp.where(k == 0, 2, 2 * k - 1))
        dx = jnp.where(early, 0, dx)
        second = jnp.where(early, lax.rem(s, 2), second)
        xx = lax.rem(x + dx, NX)
        first = 2 * second + g
        dys = [first, lax.rem(first + 1, NY)]
        yys = [lax.rem(y + dy, NY) for dy in dys]
        return g, dx, xx, dys, yys

    def wait_queries(g, xx, dys, yys):
        for dy, yy in zip(dys, yys):

            @pl.when(dy != 0)
            def _():
                q_wait(g, xx, yy)

    def step(it, carry):
        g, dx, xx, dys, yys = plan(it)
        next_g, _, next_xx, next_dys, next_yys = plan(jnp.minimum(it + 1, 8 * PHASES - 1))

        @pl.when(it == 0)
        def _():
            for dx in (2, 1, 3):
                q_wait(0, lax.rem(x + dx, NX), y)
                for d in range(1 if dx == 2 else 2, 4):
                    q_along_y(0, dx, d).start()
            for d in (2, 1, 3):
                q_along_x(1, d).start()

        @pl.when(it == 3)
        def _():
            for dx in (2, 1, 3):
                q_wait(1, lax.rem(x + dx, NX), y)
                for d in range(1, 4):
                    q_along_y(1, dx, d).start()

        @pl.when(it == 5)
        def _():
            for d in range(1, 4):
                q_along_y(1, 0, d).start()

        @pl.when(it + 1 < 8 * PHASES)
        def _():
            wait_queries(next_g, next_xx, next_dys, next_yys)

        attend(g, [q_block(xx, yy) for yy in yys], next_g, [q_block(next_xx, yy) for yy in next_yys])

        @pl.when(dx != 0)
        def _():
            for yy in yys:
                x_copy(g, dx, yy).start()

        @pl.when((it == 9) | (it == 14))
        def _():
            for dy in (1, 2):
                add_along_x(lax.div(it - 9, 5), dy)

        @pl.when(it == 9)
        def _():
            add_along_x(0, 3)

        @pl.when(it == 13)
        def _():
            add_along_y(0)

        return carry

    q_wait(0, x, lax.rem(y + 1, NY))
    first_top[...] = scores(0, [own, q_block(x, lax.rem(y + 1, NY))], 0, 0)
    lax.fori_loop(0, 8 * PHASES, step, 0)

    add_along_x(1, 3)
    for i in range(HEADS):
        wo_wait(i)
    mix[...] = add_along_z(0)
    add_along_y(1)
    mix[...] += add_along_z(1)
    core_copy = pltpu.make_async_remote_copy(
        src_ref=mix.at[pl.ds(pl.multiple_of((1 - c) * 8, 8), 8)], dst_ref=mix_in,
        send_sem=core_sem.at[0], recv_sem=core_sem.at[1], device_id=other, device_id_type=MESH,
    )
    core_copy.start()

    q_across(0, 3).wait_send()
    q_across(1, 1).wait_send()
    for g in range(PHASES):
        for d in range(1, 4):
            q_along_x(g, d).wait_send()
            y_copy(g, d).wait_send()
            for yy in range(NY):
                x_copy(g, d, yy).wait_send()
            for dx in range(NX):
                if (g, d, dx % 2) != (0, 1, 1):
                    q_along_y(g, dx, d).wait_send()
        for dz in range(1, NZ):
            z_copy(g, dz).wait_send()
    for dz in range(1, NZ):
        wo_copy(dz).wait_send()

    @pl.when(c != group)
    def _():
        wo_copy(0).wait_send()

    core_copy.wait()
    out_ref[...] = (mix[pl.ds(pl.multiple_of(c * 8, 8), 8), :] + mix_in[...]).astype(BF)


def local(context, latents, ends, w_query, w_key, w_value, w_out):
    dma = pltpu.SemaphoreType.DMA
    vmem = pltpu.VMEM
    hbm = pl.BlockSpec(memory_space=pl.ANY)
    return pl.pallas_call(
        kernel,
        out_shape=jax.ShapeDtypeStruct((8, 2 * FEAT), BF),
        in_specs=[hbm, hbm, pl.BlockSpec(memory_space=vmem), hbm, hbm, hbm, hbm],
        out_specs=pl.BlockSpec(memory_space=vmem),
        scratch_shapes=[
            vmem((POS, 1024), BF),
            vmem((ROWS, 1024), BF),
            vmem((1024, FEAT), BF),
            vmem((1024, FEAT), BF),
            vmem((1024, FEAT), BF),
            vmem((FEAT, 1024), BF),
            vmem((PHASES, NX * NY, WIDE, ROWS), BF),
            vmem((PHASES, POS, 128 * GROUP), BF),
            vmem((PHASES, VROWS * GROUP, POS), BF),
            vmem((PHASES, NX * NY, PAY, ROWS), BF),
            vmem((PHASES, 3, NY, PAY, ROWS), BF),
            vmem((PHASES, 3, PAY, ROWS), BF),
            vmem((PHASES, 3, PAY, ROWS), BF),
            vmem((PHASES, ROWS, WIDE + 128), BF),
            vmem((PHASES, NZ, OWN, WIDE + 128), BF),
            vmem((OWN, 1024), F32),
            vmem((8, 1024), F32),
            vmem((2, POS, 2 * ROWS), F32),
            vmem((1, 2 * ROWS), F32),
            dma((5,)), dma((2,)), dma((NZ,)), dma((HEADS,)),
            dma((PHASES, 3)), dma((2,)), dma((PHASES, NX, 3)), dma((PHASES, NX * NY)),
            dma((PHASES, 3, NY)), dma((PHASES, 3, NY)), dma((PHASES, 3)), dma((PHASES, 3)),
            dma((PHASES, NZ)), dma((PHASES, NZ)), dma((2,)),
        ],
        compiler_params=pltpu.CompilerParams(
            collective_id=0, has_side_effects=True, vmem_limit_bytes=63 * 2**20
        ),
        name="attend",
    )(context, latents, ends.reshape(NX * NY, ROWS), w_query, w_key, w_value, w_out)


def solution(mesh):
    in_specs = (P(("major", "minor"), None), P("major", None), P(), P(), P(), P(), P("minor", None))
    out_specs = P(("major", "minor"), None)
    return jax.shard_map(local, mesh=mesh, in_specs=in_specs, out_specs=out_specs, check_vma=False)
```

```python
import math

import jax
import jax.numpy as jnp
from jax import lax
from jax.experimental import pallas as pl
from jax.experimental.pallas import tpu as pltpu
from jax.sharding import PartitionSpec as P

HEAD = 64
NX, NY, NZ = 4, 4, 8
HEADS = 8
FEAT = HEADS * HEAD
PHASES = 2
GROUP = HEADS // PHASES
WIDE = GROUP * HEAD
TOK = 512
POS = 2 * TOK
ROWS = 128
PART = 128
OWN = 2 * 8
VROWS = 80
PAY = WIDE + 16
LOG2E = math.log2(math.e)
NEG = -1e30
MESH = pl.DeviceIdType.MESH
BF = jnp.bfloat16
F32 = jnp.float32


def split3(a):
    hi = a.astype(BF)
    rest = a - hi.astype(F32)
    mid = rest.astype(BF)
    low = (rest - mid.astype(F32)).astype(BF)
    return hi, mid, low


def stats_of(pay):
    rows = pay[WIDE:, :].astype(F32)
    top = rows[:GROUP] + rows[GROUP : 2 * GROUP] + rows[2 * GROUP : 3 * GROUP]
    return jnp.concatenate([top, rows[3 * GROUP :]], axis=0)


def stats_rows(stats):
    terms = [t.astype(F32) for t in split3(stats[:GROUP])]
    return jnp.concatenate(terms + [stats[GROUP:]], axis=0)


def merge(pays):
    stats = [stats_of(pay) for pay in pays]
    top = stats[0][:GROUP]
    for st in stats[1:]:
        top = jnp.maximum(top, st[:GROUP])
    factors = [jnp.exp2(st[:GROUP] - top) for st in stats]
    den = sum(f * st[GROUP:] for f, st in zip(factors, stats))
    nums = []
    for h in range(GROUP):
        rows = slice(h * HEAD, h * HEAD + HEAD)
        nums.append(sum(pay[rows, :].astype(F32) * f[h : h + 1, :] for f, pay in zip(factors, pays)))
    return nums, jnp.concatenate([top, den], axis=0)


def write_payload(dst, nums, stats):
    for h in range(GROUP):
        dst[h * HEAD : h * HEAD + HEAD, :] = nums[h].astype(BF)
    dst[WIDE:, :] = stats_rows(stats).astype(BF)


def kernel(
    ctx_ref, lat_ref, ends_ref, wq_ref, wk_ref, wv_ref, wo_ref, out_ref,
    ctx, lat, wq, wk, wv, wo, qt, kk, vt, part, recv_x, sum_y, recv_y, zsend, zbuf, mix, mix_in, held, first_top,
    load_sem, ctx_sem, wo_send, wo_recv, qx_send, qd_send, qy_send, q_recv,
    x_send, x_recv, y_send, y_recv, z_send, z_recv, core_sem,
):
    major, minor = lax.axis_index("major"), lax.axis_index("minor")
    x, y = lax.div(major, NY), lax.rem(major, NY)
    z, c = lax.div(minor, 2), lax.rem(minor, 2)

    def at_x(d):
        return (lax.rem(x + d, NX) * NY + y, minor)

    def at_y(d):
        return (x * NY + lax.rem(y + d, NY), minor)

    def at_xy(d, e):
        return (lax.rem(x + d, NX) * NY + lax.rem(y + e, NY), minor)

    other = (major, 2 * z + 1 - c)
    half = pl.ds(pl.multiple_of(c * FEAT, FEAT), FEAT)
    mine = pl.ds(pl.multiple_of(c * TOK, TOK), TOK)
    theirs = pl.ds(pl.multiple_of((1 - c) * TOK, TOK), TOK)

    loads = [
        pltpu.make_async_copy(lat_ref, lat, load_sem.at[0]),
        pltpu.make_async_copy(wq_ref.at[:, half], wq, load_sem.at[1]),
        pltpu.make_async_copy(ctx_ref, ctx.at[mine], load_sem.at[2]),
        pltpu.make_async_copy(wk_ref.at[:, half], wk, load_sem.at[3]),
        pltpu.make_async_copy(wv_ref.at[:, half], wv, load_sem.at[4]),
    ]
    for load in loads:
        load.start()

    barrier = pltpu.get_barrier_semaphore()
    for d in range(1, 4):
        pl.semaphore_signal(barrier, inc=1, device_id=at_x(d), device_id_type=MESH)
        pl.semaphore_signal(barrier, inc=1, device_id=at_y(d), device_id_type=MESH)
    for d in (1, 3):
        for e in (1, 3):
            pl.semaphore_signal(barrier, inc=1, device_id=at_xy(d, e), device_id_type=MESH)
    for d in range(1, 16):
        pl.semaphore_signal(barrier, inc=1, device_id=(major, lax.rem(minor + d, 16)), device_id_type=MESH)

    def q_block(xx, yy):
        return xx * NY + yy

    own = q_block(x, y)
    loads[0].wait()
    loads[1].wait()
    q = jnp.dot(lat[...], wq[...], preferred_element_type=F32) * HEAD ** (-0.5)
    q = jnp.transpose(q.astype(BF).astype(F32)).astype(BF)
    for g in range(PHASES):
        qt[g, own] = q[g * WIDE : (g + 1) * WIDE, :]

    pl.semaphore_wait(barrier, 25)
    ctx_copy = pltpu.make_async_remote_copy(
        src_ref=ctx_ref, dst_ref=ctx.at[mine], send_sem=ctx_sem.at[0], recv_sem=ctx_sem.at[1],
        device_id=other, device_id_type=MESH,
    )
    ctx_copy.start()

    def q_copy(g, block, send_sem, device):
        return pltpu.make_async_remote_copy(
            src_ref=qt.at[g, block], dst_ref=qt.at[g, block], send_sem=send_sem, recv_sem=q_recv.at[g, block],
            device_id=device, device_id_type=MESH,
        )

    def q_along_x(g, d):
        return q_copy(g, own, qx_send.at[g, d - 1], at_x(NX - d))

    def q_along_y(g, dx, d):
        return q_copy(g, q_block(lax.rem(x + dx, NX), y), qy_send.at[g, dx, d - 1], at_y(NY - d))

    def q_across(i, d):
        return q_copy(0, own, qd_send.at[i], at_xy(d, NY - 1))

    def q_wait(g, xx, yy):
        q_copy(g, q_block(xx, yy), qx_send.at[0, 0], other).wait_recv()

    q_along_y(0, 0, 1).start()
    q_along_x(0, 1).start()
    q_along_x(0, 3).start()
    q_across(0, 3).start()
    q_across(1, 1).start()
    q_along_y(0, 0, 2).start()
    q_along_y(0, 0, 3).start()
    q_along_x(0, 2).start()

    lane = lax.broadcasted_iota(jnp.int32, (TOK, 128), 1)

    def project_keys(rows):
        keys = jnp.dot(ctx[rows, :], wk[...], preferred_element_type=F32).astype(BF).astype(F32) * LOG2E
        hi = keys.astype(BF).astype(F32)
        low = (keys - hi).astype(BF).astype(F32)
        for pair in range(HEADS // 2):
            cols = slice(pair * 128, pair * 128 + 128)
            a, b = hi[:, cols], low[:, cols]
            even = jnp.where(lane < HEAD, a, pltpu.roll(b, HEAD, 1))
            odd = jnp.where(lane < HEAD, pltpu.roll(a, HEAD, 1), b)
            g, start = divmod(2 * pair, GROUP)
            kk[g, rows, start * 128 : start * 128 + 128] = even.astype(BF)
            kk[g, rows, start * 128 + 128 : start * 128 + 256] = odd.astype(BF)

    def project_values(rows):
        values = jnp.dot(ctx[rows, :], wv[...], preferred_element_type=F32).astype(BF).astype(F32)
        turned = jnp.transpose(values).astype(BF)
        for h in range(HEADS):
            g, i = divmod(h, GROUP)
            vt[g, i * VROWS : i * VROWS + HEAD, rows] = turned[h * HEAD : h * HEAD + HEAD, :]

    loads[2].wait()
    loads[3].wait()
    project_keys(mine)


    group, place = lax.div(minor, HEADS), lax.rem(minor, HEADS)
    wo_rows = pl.ds(pl.multiple_of(place * HEAD, HEAD), HEAD)

    def wo_copy(dz):
        return pltpu.make_async_remote_copy(
            src_ref=wo_ref, dst_ref=wo.at[wo_rows], send_sem=wo_send.at[dz], recv_sem=wo_recv.at[place],
            device_id=(major, lax.rem(z + dz, NZ) * 2 + group), device_id_type=MESH,
        )

    wo_local = pltpu.make_async_copy(wo_ref, wo.at[wo_rows], wo_recv.at[place])
    for dz in range(1, NZ):
        wo_copy(dz).start()

    @pl.when(c == group)
    def _():
        wo_local.start()

    @pl.when(c != group)
    def _():
        wo_copy(0).start()

    loads[4].wait()
    project_values(mine)
    row16 = lax.broadcasted_iota(jnp.int32, (16, POS), 0)
    for h in range(HEADS):
        g, i = divmod(h, GROUP)
        vt[g, i * VROWS + HEAD : (i + 1) * VROWS, :] = jnp.where(row16 == 0, 1.0, 0.0).astype(BF)

    ctx_copy.wait()
    project_keys(theirs)
    project_values(theirs)

    def x_copy(g, dx, yy):
        return pltpu.make_async_remote_copy(
            src_ref=part.at[g, q_block(lax.rem(x + dx, NX), yy)], dst_ref=recv_x.at[g, dx - 1, yy],
            send_sem=x_send.at[g, dx - 1, yy], recv_sem=x_recv.at[g, dx - 1, yy],
            device_id=at_x(dx), device_id_type=MESH,
        )

    def y_copy(g, dy):
        return pltpu.make_async_remote_copy(
            src_ref=sum_y.at[g, dy - 1], dst_ref=recv_y.at[g, dy - 1], send_sem=y_send.at[g, dy - 1],
            recv_sem=y_recv.at[g, dy - 1], device_id=at_y(dy), device_id_type=MESH,
        )

    def add_along_x(g, dy):
        yy = lax.rem(y + dy, NY)
        for d in range(1, 4):
            x_copy(g, d, yy).wait_recv()
        write_payload(sum_y.at[g, dy - 1], *merge([part.at[g, q_block(x, yy)]] + [recv_x.at[g, d, yy] for d in range(3)]))
        y_copy(g, dy).start()

    def z_rows(dz):
        return pl.ds(pl.multiple_of(lax.rem(z + dz, NZ) * OWN, OWN), OWN)

    def z_copy(g, dz):
        return pltpu.make_async_remote_copy(
            src_ref=zsend.at[g, z_rows(dz)], dst_ref=zbuf.at[g, z], send_sem=z_send.at[g, dz],
            recv_sem=z_recv.at[g, z], device_id=(major, lax.rem(z + dz, NZ) * 2 + c), device_id_type=MESH,
        )

    def add_along_y(g):
        for d in range(1, 4):
            x_copy(g, d, y).wait_recv()
        for d in range(1, 4):
            y_copy(g, d).wait_recv()
        nums, stats = merge(
            [part.at[g, own]] + [recv_x.at[g, d, y] for d in range(3)] + [recv_y.at[g, d] for d in range(3)]
        )
        zsend[g, :, :WIDE] = jnp.transpose(jnp.concatenate(nums, axis=0)).astype(BF)
        rows = jnp.concatenate([stats_rows(stats), jnp.zeros((112, ROWS), F32)], axis=0)
        zsend[g, :, WIDE:] = jnp.transpose(rows).astype(BF)
        for dz in (4, 3, 5, 2, 6, 1, 7):
            z_copy(g, dz).start()
        pltpu.make_async_copy(zsend.at[g, z_rows(0)], zbuf.at[g, z], z_recv.at[g, z]).start()

    def add_along_z(g):
        head_of = lax.shift_right_logical(lax.broadcasted_iota(jnp.int32, (128, WIDE), 1), 6)
        line = lax.broadcasted_iota(jnp.int32, (128, WIDE), 0)
        spread = jnp.where(head_of == line, 1.0, 0.0).astype(BF)
        spread_den = jnp.where(head_of == line - 3 * GROUP, 1.0, 0.0).astype(BF)
        lane16 = lax.broadcasted_iota(jnp.int32, (OWN, 128), 1)
        for i in range(NZ):
            pltpu.make_async_copy(zsend.at[g, pl.ds(0, OWN)], zbuf.at[g, i], z_recv.at[g, i]).wait()
        sums = [zbuf[g, i, :, WIDE:].astype(F32) for i in range(NZ)]
        tops = [t + pltpu.roll(t, 128 - GROUP, 1) + pltpu.roll(t, 128 - 2 * GROUP, 1) for t in sums]
        top = tops[0]
        for t in tops[1:]:
            top = jnp.maximum(top, t)
        factors = [jnp.where(lane16 < GROUP, jnp.exp2(t - top), 0.0) for t in tops]
        wide = jnp.dot(jnp.concatenate(factors, axis=0).astype(BF), spread, preferred_element_type=F32)
        num = sum(wide[i * OWN : i * OWN + OWN] * zbuf[g, i, :, :WIDE].astype(F32) for i in range(NZ))
        den = sum(pltpu.roll(f, 3 * GROUP, 1) * t for f, t in zip(factors, sums))
        den_wide = sum(jnp.dot(t, spread_den, preferred_element_type=F32) for t in split3(den))
        attended = (num / den_wide).astype(BF)
        return jnp.dot(attended, wo[g * WIDE : (g + 1) * WIDE, :], preferred_element_type=F32)

    def wo_wait(i):
        pltpu.make_async_copy(wo_ref, wo.at[pl.ds(i * HEAD, HEAD)], wo_recv.at[i]).wait()

    base = (major * 16 + 2 * z) * TOK
    place_in_part = lax.broadcasted_iota(jnp.int32, (PART, 2 * ROWS), 0)

    def scores(g, blocks, h, slot):
        ends = jnp.concatenate([ends_ref[pl.ds(b, 1), :] for b in blocks], axis=1) - base
        rows = slice(h * HEAD, h * HEAD + HEAD)
        qh = jnp.concatenate([qt[g, b, rows, :] for b in blocks], axis=1)
        qh = jnp.concatenate([qh, qh], axis=0)
        top = None
        for j in range(0, POS, PART):
            keys = kk[g, j : j + PART, h * 128 : h * 128 + 128]
            now = jnp.dot(keys, qh, preferred_element_type=F32)
            now = jnp.where(place_in_part < ends - j, now, NEG)
            held[slot, j : j + PART, :] = now
            most = jnp.max(now.reshape(PART // 8, 8, 2 * ROWS), axis=0)
            top = most if top is None else jnp.maximum(top, most)
        return jnp.ceil(jnp.max(top, axis=0, keepdims=True))

    def attend(g, blocks, next_g, next_blocks):
        tops, dens = [], []
        top = first_top[...]
        for h in range(GROUP):
            if h + 1 < GROUP:
                next_top = scores(g, blocks, h + 1, (h + 1) % 2)
            else:
                next_top = scores(next_g, next_blocks, 0, 0)
                first_top[...] = next_top
            probs = [
                jnp.exp2(held[h % 2, j : j + PART, :] - top).astype(BF) for j in range(0, POS, PART)
            ]
            probs = jnp.concatenate(probs, axis=0)
            res = jnp.dot(vt[g, h * VROWS : (h + 1) * VROWS, :], probs, preferred_element_type=F32)
            for i, b in enumerate(blocks):
                part[g, b, h * HEAD : h * HEAD + HEAD, :] = res[:HEAD, i * ROWS : i * ROWS + ROWS].astype(BF)
            tops.append(top)
            dens.append(res[HEAD : HEAD + 1, :])
            top = next_top
        rows = stats_rows(jnp.concatenate(tops + dens, axis=0)).astype(BF)
        for i, b in enumerate(blocks):
            part[g, b, WIDE:, :] = rows[:, i * ROWS : i * ROWS + ROWS]

    def plan(it):
        g, s = lax.div(it, 8), lax.rem(it, 8)
        early = jnp.where(g == 0, s < 2, s >= 6)
        t = jnp.where(g == 0, s + 4, s)
        k, second = lax.rem(t, 3), jnp.where(g == 0, lax.div(t - 6, 3), lax.div(t, 3))
        dx = jnp.where(g == 0, jnp.where(k == 2, 2, 1 + 2 * k), jnp.where(k == 0, 2, 2 * k - 1))
        dx = jnp.where(early, 0, dx)
        second = jnp.where(early, lax.rem(s, 2), second)
        xx = lax.rem(x + dx, NX)
        first = 2 * second + g
        dys = [first, lax.rem(first + 1, NY)]
        yys = [lax.rem(y + dy, NY) for dy in dys]
        return g, dx, xx, dys, yys

    def wait_queries(g, xx, dys, yys):
        for dy, yy in zip(dys, yys):

            @pl.when(dy != 0)
            def _():
                q_wait(g, xx, yy)

    def step(it, carry):
        g, dx, xx, dys, yys = plan(it)
        next_g, _, next_xx, next_dys, next_yys = plan(jnp.minimum(it + 1, 8 * PHASES - 1))

        @pl.when(it == 0)
        def _():
            for dx in (2, 1, 3):
                q_wait(0, lax.rem(x + dx, NX), y)
                for d in range(1 if dx == 2 else 2, 4):
                    q_along_y(0, dx, d).start()
        @pl.when(it == 2)
        def _():
            for d in (2, 1, 3):
                q_along_x(1, d).start()

        @pl.when(it == 4)
        def _():
            for dx in (2, 1, 3):
                q_wait(1, lax.rem(x + dx, NX), y)
                for d in range(1, 4):
                    q_along_y(1, dx, d).start()

        @pl.when(it == 6)
        def _():
            for d in range(1, 4):
                q_along_y(1, 0, d).start()

        @pl.when(it + 1 < 8 * PHASES)
        def _():
            wait_queries(next_g, next_xx, next_dys, next_yys)

        attend(g, [q_block(xx, yy) for yy in yys], next_g, [q_block(next_xx, yy) for yy in next_yys])

        @pl.when(dx != 0)
        def _():
            for yy in yys:
                x_copy(g, dx, yy).start()

        @pl.when((it == 9) | (it == 14))
        def _():
            for dy in (1, 2):
                add_along_x(lax.div(it - 9, 5), dy)

        @pl.when(it == 9)
        def _():
            add_along_x(0, 3)

        @pl.when(it == 13)
        def _():
            add_along_y(0)

        return carry

    q_wait(0, x, lax.rem(y + 1, NY))
    first_top[...] = scores(0, [own, q_block(x, lax.rem(y + 1, NY))], 0, 0)
    lax.fori_loop(0, 8 * PHASES, step, 0)

    add_along_x(1, 3)
    for i in range(HEADS):
        wo_wait(i)
    mix[...] = add_along_z(0)
    add_along_y(1)
    mix[...] += add_along_z(1)
    core_copy = pltpu.make_async_remote_copy(
        src_ref=mix.at[pl.ds(pl.multiple_of((1 - c) * 8, 8), 8)], dst_ref=mix_in,
        send_sem=core_sem.at[0], recv_sem=core_sem.at[1], device_id=other, device_id_type=MESH,
    )
    core_copy.start()

    q_across(0, 3).wait_send()
    q_across(1, 1).wait_send()
    for g in range(PHASES):
        for d in range(1, 4):
            q_along_x(g, d).wait_send()
            y_copy(g, d).wait_send()
            for yy in range(NY):
                x_copy(g, d, yy).wait_send()
            for dx in range(NX):
                if (g, d, dx % 2) != (0, 1, 1):
                    q_along_y(g, dx, d).wait_send()
        for dz in range(1, NZ):
            z_copy(g, dz).wait_send()
    for dz in range(1, NZ):
        wo_copy(dz).wait_send()

    @pl.when(c != group)
    def _():
        wo_copy(0).wait_send()

    core_copy.wait()
    out_ref[...] = (mix[pl.ds(pl.multiple_of(c * 8, 8), 8), :] + mix_in[...]).astype(BF)


def local(context, latents, ends, w_query, w_key, w_value, w_out):
    dma = pltpu.SemaphoreType.DMA
    vmem = pltpu.VMEM
    hbm = pl.BlockSpec(memory_space=pl.ANY)
    return pl.pallas_call(
        kernel,
        out_shape=jax.ShapeDtypeStruct((8, 2 * FEAT), BF),
        in_specs=[hbm, hbm, pl.BlockSpec(memory_space=vmem), hbm, hbm, hbm, hbm],
        out_specs=pl.BlockSpec(memory_space=vmem),
        scratch_shapes=[
            vmem((POS, 1024), BF),
            vmem((ROWS, 1024), BF),
            vmem((1024, FEAT), BF),
            vmem((1024, FEAT), BF),
            vmem((1024, FEAT), BF),
            vmem((FEAT, 1024), BF),
            vmem((PHASES, NX * NY, WIDE, ROWS), BF),
            vmem((PHASES, POS, 128 * GROUP), BF),
            vmem((PHASES, VROWS * GROUP, POS), BF),
            vmem((PHASES, NX * NY, PAY, ROWS), BF),
            vmem((PHASES, 3, NY, PAY, ROWS), BF),
            vmem((PHASES, 3, PAY, ROWS), BF),
            vmem((PHASES, 3, PAY, ROWS), BF),
            vmem((PHASES, ROWS, WIDE + 128), BF),
            vmem((PHASES, NZ, OWN, WIDE + 128), BF),
            vmem((OWN, 1024), F32),
            vmem((8, 1024), F32),
            vmem((2, POS, 2 * ROWS), F32),
            vmem((1, 2 * ROWS), F32),
            dma((5,)), dma((2,)), dma((NZ,)), dma((HEADS,)),
            dma((PHASES, 3)), dma((2,)), dma((PHASES, NX, 3)), dma((PHASES, NX * NY)),
            dma((PHASES, 3, NY)), dma((PHASES, 3, NY)), dma((PHASES, 3)), dma((PHASES, 3)),
            dma((PHASES, NZ)), dma((PHASES, NZ)), dma((2,)),
        ],
        compiler_params=pltpu.CompilerParams(
            collective_id=0, has_side_effects=True, vmem_limit_bytes=63 * 2**20
        ),
        name="attend",
    )(context, latents, ends.reshape(NX * NY, ROWS), w_query, w_key, w_value, w_out)


def solution(mesh):
    in_specs = (P(("major", "minor"), None), P("major", None), P(), P(), P(), P(), P("minor", None))
    out_specs = P(("major", "minor"), None)
    return jax.shard_map(local, mesh=mesh, in_specs=in_specs, out_specs=out_specs, check_vma=False)
```
